512 devices in a mesh: dp: 16 (over x, z_hi), section: 32 (over y, z_lo, core).
Axes of the slice: x: 4, y: 8, z: 8 (z_hi: 4, z_lo: 2; z = z_hi * 2 + z_lo), core: 2. Of those that a mesh axis runs over, the one named last changes fastest.
Arguments:
- upstream: bfloat16 [32, 3, 768, 6656], P('section', None, 'dp'), may hold values from -6 to 6
- inputs: bfloat16 [32, 3, 768, 128], P('section', None, 'dp'), may hold values from -6 to 6
- in_proj: bfloat16 [32, 6656, 128], P('section', 'dp'), may hold values from -0.078125 to 0.078125
- out_proj: bfloat16 [32, 6656, 128], P('section', 'dp'), may hold values from -0.5 to 0.5
- in_inverse: float32 [32, 128, 128], P('section'), may hold values from -1 to 15, as said below
- out_inverse: float32 [32, 32, 208, 208], P('section', 'dp'), may hold values from -1 to 15, as said below
- lengths: int32 [32, 16, 3], P('section', 'dp'), may hold values from 1 to 48
Outputs:
- passed: bfloat16 [32, 3, 768, 6656], P('section', None, 'dp')
- precond: float32 [32, 6656, 128], P('section', 'dp')
- in_factor: float32 [32, 128, 128], P('section')
- out_factor: float32 [32, 32, 208, 208], P('section', 'dp')
The draws below stay inside these ranges and needn't reach their ends.
Inputs may be any that keep to these rules, and one draw needn't show every extreme that they name: `in_inverse`: each 128 x 128 matrix is symmetric. `out_inverse`: each 208 x 208 block is symmetric.
All inputs are finite; a program needn't handle non-finite values.
Results may differ from the reference program's by a relative error of at most 0.0039.
Values may be sent and summed in bfloat16 or wider, within the bound.
A program may use at most 64 MiB of HBM per device.

```python
import jax
import jax.numpy as jnp
from jax import lax

D = 6656
HEAD = 128
BLK = 208
MB = 3
TOK = 48
TOKENS_MB = 768
SECTIONS = 32
N_DP = 16


def symmetric_blocks(key, shape, size, spread):
    first, second, third = jax.random.split(key, 3)
    raw = jax.random.uniform(first, shape, jnp.float32, -1.0, 1.0)
    mirrored = (raw + jnp.swapaxes(raw, -1, -2)) * (0.38 / size)
    diagonal = jax.random.uniform(second, shape[:-1], jnp.float32, 0.8, 1.6)
    identity = jnp.eye(size, dtype=jnp.float32)
    base = mirrored * (1.0 - identity) + identity * diagonal[..., None]
    scales = jax.random.uniform(third, shape[:-1], jnp.float32, 1.0, spread)
    return base * scales[..., :, None] * scales[..., None, :]


def draw_in_inverse(key, part):
    key = jax.random.fold_in(key, 11)
    spread = 1.0
    return symmetric_blocks(key, (SECTIONS, HEAD, HEAD), HEAD, spread)


def draw_out_inverse(key, part):
    key = jax.random.fold_in(key, 23)
    spread = 1.0
    return symmetric_blocks(key, (SECTIONS, D // BLK, BLK, BLK), BLK, spread)


def place_ends(entries, stream_key, low, largest):
    dims = entries.shape
    index_at = [jax.random.randint(jax.random.fold_in(stream_key, axis), (), 0, dims[axis]) for axis in range(len(dims))]
    entries = entries.at[tuple(index_at)].set(low)
    longest = dims.index(max(dims))
    index_at[longest] = (index_at[longest] + 1) % dims[longest]
    return entries.at[tuple(index_at)].set(largest)


def raised(array, rng, source, target, parts, factor):
    owner, partner = [(jnp.arange(array.shape[axis_at]) // (array.shape[axis_at] // parts)).reshape([-1 if axis == axis_at else 1 for axis in range(array.ndim)]) for axis_at in (source, target)]
    chosen = jax.random.permutation(rng, parts)[partner]
    strong = (owner == chosen) | (owner == (partner + parts // 2) % parts)
    return jnp.where(strong, factor * array, array)


def steps_of(stream_key, extent, shards, least, largest):
    def one(dim, blocks):
        draws = jax.random.uniform(jax.random.fold_in(jax.random.fold_in(stream_key, 6), dim), (blocks,), jnp.float32, least / len(shards), largest / len(shards))
        return jnp.repeat(jnp.exp(draws), extent[dim] // blocks).reshape((-1,) + (1,) * (len(extent) - dim - 1))

    loudness = one(*shards[0])
    for cut in shards[1:]:
        loudness = loudness * one(*cut)
    return loudness


def normal_values(rng, extent, scale, most, pieces=(), kind=jnp.bfloat16):
    entries = jax.random.normal(rng, extent, jnp.float32) * scale
    if len(pieces) > 0:
        entries = steps_of(rng, extent, pieces, -0.22, 0.18) * entries
    return jnp.clip(entries, min=-most, max=most).astype(kind)


def gaussian_with(own_key, shape, scale, reach, cuts, heavy, kind=jnp.bfloat16):
    values = scale * jax.random.normal(own_key, shape, jnp.float32)
    if cuts:
        values = values * steps_of(own_key, shape, cuts, -0.22, 0.18)
    return jnp.clip(raised(values, jax.random.fold_in(own_key, 3), *heavy), -reach, reach).astype(kind)


def setup_inputs(seed: int = 0) -> dict:
    arg_keys = jax.random.split(jax.random.key(seed), 8)
    upstream = gaussian_with(arg_keys[0], (SECTIONS, MB, TOKENS_MB, D), 1.0, 6.0, ((0, 32), (2, 16)), (2, 3, 16, 2.0))
    inputs = normal_values(arg_keys[1], (SECTIONS, MB, TOKENS_MB, HEAD), 1.0, 6.0, ((0, 32), (2, 16)))
    in_proj = normal_values(arg_keys[2], (SECTIONS, D, HEAD), D ** -0.5, 0.078125, ((0, 32), (1, 16)))
    out_proj = normal_values(arg_keys[3], (SECTIONS, D, HEAD), HEAD ** -0.5, 0.5, ((0, 32), (1, 16)))
    in_inverse = draw_in_inverse(jax.random.fold_in(arg_keys[7], 71), 0)
    out_inverse = draw_out_inverse(jax.random.fold_in(arg_keys[7], 71), 0)
    lengths = place_ends(jax.random.randint(arg_keys[6], (SECTIONS, N_DP, MB), 1, TOK + 1), jax.random.fold_in(arg_keys[6], 1), 1, TOK).astype(jnp.int32)
    return dict(upstream=upstream, inputs=inputs, in_proj=in_proj, out_proj=out_proj, in_inverse=in_inverse, out_inverse=out_inverse, lengths=lengths)


def section_work(upstream, inputs, in_proj, out_proj, in_inverse, out_inverse, lengths):
    batches, total_rows, width = upstream.shape
    rows = total_rows // N_DP
    position = jnp.arange(total_rows, dtype=jnp.int32)
    owner = position // rows
    offset = position % rows
    limit = lengths[owner, :]
    keep = (offset[None, :] < limit.T).astype(jnp.bfloat16)[:, :, None]
    grads = upstream * keep
    values = inputs * keep
    flat_grads = grads.reshape(batches * total_rows, width)
    flat_values = values.reshape(batches * total_rows, HEAD)
    branch = jnp.dot(flat_grads, out_proj, preferred_element_type=jnp.float32).astype(jnp.bfloat16)
    act_grad = flat_grads.astype(jnp.float32) + jnp.dot(branch, in_proj.T, preferred_element_type=jnp.float32)
    act_grad = act_grad.astype(jnp.bfloat16).reshape(batches, total_rows, width)
    count = jnp.sum(lengths).astype(jnp.float32)
    in_factor = jnp.dot(flat_values.T, flat_values, preferred_element_type=jnp.float32) / count
    stacked = flat_grads.reshape(batches * total_rows, D // BLK, BLK).astype(jnp.float32)
    out_factor = jnp.einsum('tbi,tbj->bij', stacked, stacked, precision=lax.Precision.HIGHEST) / count
    weight_grad = jnp.dot(flat_grads.T, flat_values, preferred_element_type=jnp.float32) / jnp.sqrt(count)
    left = jnp.einsum('bij,bjh->bih', out_inverse, weight_grad.reshape(D // BLK, BLK, HEAD), precision=lax.Precision.HIGHEST)
    precond = jnp.dot(left.reshape(D, HEAD), in_inverse, precision=lax.Precision.HIGHEST)
    return (act_grad, precond, in_factor, out_factor)

def reference(upstream, inputs, in_proj, out_proj, in_inverse, out_inverse, lengths):

    def one_section(operands):
        return section_work(*operands)
    act_grad, precond, in_factor, out_factor = lax.map(one_section, (upstream, inputs, in_proj, out_proj, in_inverse, out_inverse, lengths))
    passed = jnp.concatenate([act_grad[1:], jnp.zeros_like(act_grad[:1])], axis=0)
    return (passed, precond, in_factor, out_factor)
```

```python
import functools

import jax
import jax.numpy as jnp
from jax import lax
from jax.experimental import pallas as pl
from jax.experimental.pallas import tpu as pltpu
from jax.sharding import PartitionSpec as P

RING = 4
BF16 = jnp.bfloat16
F32 = jnp.float32


def nt_dot(a, b):
    return lax.dot_general(a, b, (((1,), (1,)), ((), ())), preferred_element_type=F32)


def tn_dot(a, b):
    return lax.dot_general(a, b, (((0,), (0,)), ((), ())), preferred_element_type=F32)


def kernel(
    lengths, upstream, inputs, in_proj, out_proj, in_inverse, out_inverse,
    passed, precond, in_factor, out_factor,
    grads, split, split_t, relayed, values, out_rows, in_rows, partial, partial_in, branch, branch_in,
    stats, stats_in, split_send, split_recv, value_send, value_recv, out_send, out_recv,
    relay_send, relay_recv, in_send, in_recv, partial_send, partial_recv, stats_send, stats_recv,
):
    rows, width = upstream.shape
    slots = rows // lengths.shape[0]
    shard = in_proj.shape[0]
    blocks, size, _ = out_inverse.shape
    head = in_proj.shape[1]
    span = RING * shard
    sections = lax.axis_size("section")
    dp = lax.axis_index("dp")
    section = lax.axis_index("section")
    x = lax.div(dp, RING)
    z = lax.rem(dp, RING)
    before = {"section": lax.rem(section + sections - 1, sections)}
    after = {"section": lax.rem(section + 1, sections)}

    def along_x(r):
        return {"dp": lax.rem(x + r, RING) * RING + z}

    def along_z(r):
        return {"dp": x * RING + lax.rem(z + r, RING)}

    def send(src, dst, send_sem, recv_sem, device):
        copy = pltpu.make_async_remote_copy(
            src_ref=src, dst_ref=dst, send_sem=send_sem, recv_sem=recv_sem,
            device_id=device, device_id_type=pl.DeviceIdType.MESH,
        )
        copy.start()
        return copy

    barrier = pltpu.get_barrier_semaphore()
    for device in [along_x(r) for r in (1, 2, 3)] + [along_z(r) for r in (1, 2, 3)] + [before, after]:
        pl.semaphore_signal(barrier, inc=1, device_id=device, device_id_type=pl.DeviceIdType.MESH)

    position = lax.broadcasted_iota(jnp.int32, (rows, 1), 0)
    batch = lax.div(position, slots)
    limit = jnp.where(batch == 0, lengths[0], jnp.where(batch == 1, lengths[1], lengths[2]))
    keep = (lax.rem(position, slots) < limit).astype(F32)
    keep = jnp.broadcast_to(keep, (rows, head)).astype(BF16)
    counted = (lengths[0] + lengths[1] + lengths[2]).astype(F32)
    values[0, 0:rows, :] = inputs[...] * keep
    values[0, rows:, :] = jnp.full((values.shape[1] - rows, head), counted, F32).astype(BF16)
    own_out = pl.ds(pl.multiple_of(z * shard, 16), shard)
    out_rows[own_out, :] = out_proj[...]

    def mask(first, columns):
        for c in range(columns // head):
            where = pl.ds(pl.multiple_of(first + c * head, head), head)
            grads[:, where] = upstream[:, where] * keep

    pl.semaphore_wait(barrier, 8)

    copies = []
    outs = [send(out_proj, out_rows.at[own_out], out_send.at[r - 1], out_recv.at[r - 1], along_z(r)) for r in (1, 2, 3)]
    vals = [send(values.at[0], values.at[r], value_send.at[r - 1], value_recv.at[r - 1], along_x(r)) for r in (1, 2, 3)]
    own_in = pl.ds(pl.multiple_of(dp * shard, 16), shard)
    ins = send(in_proj, in_rows.at[own_in], in_send.at[0], in_recv.at[0], before)
    splits = {}
    for r in (2, 1, 3):
        first = lax.rem(x + r, RING) * span
        mask(first, span)
        splits[r] = send(
            grads.at[:, pl.ds(pl.multiple_of(first, head), span)], split.at[pl.ds(r * rows, rows)],
            split_send.at[r - 1], split_recv.at[r - 1], along_x(r),
        )
    mask(x * span, span)
    relay = send(grads, relayed, relay_send.at[0], relay_recv.at[0], before)
    for c in range(span // head):
        where = pl.ds(pl.multiple_of(x * span + c * head, head), head)
        split[0:rows, c * head:(c + 1) * head] = grads[:, where]

    ins.wait_recv()
    ins_z = [
        send(in_rows.at[own_in], in_rows.at[own_in], in_send.at[r], in_recv.at[r], along_z(r)) for r in (1, 2, 3)
    ]

    for copy in outs + vals:
        copy.wait_recv()
    for r in (1, 2, 3):
        splits[r].wait_recv()

    part = jnp.dot(split[...], out_rows[...], preferred_element_type=F32)
    partial[...] = part.astype(BF16)
    partials = [
        send(
            partial.at[pl.ds(r * rows, rows)], partial_in.at[r - 1],
            partial_send.at[r - 1], partial_recv.at[r - 1], along_x(RING - r),
        )
        for r in (1, 2, 3)
    ]

    split_t[...] = split[...].T
    stacked = jnp.concatenate([values[r, 0:rows, :] for r in range(RING)], axis=0)
    gram_in = tn_dot(stacked, stacked)
    count_rows = values[0, rows:, :].astype(F32)
    row = lax.broadcasted_iota(jnp.int32, count_rows.shape, 0)
    counts = jnp.zeros_like(count_rows)
    for r in range(RING):
        counts = jnp.where(row == r, values[r, rows:, :].astype(F32), counts)
    packed = size + size - head
    at_weight = blocks * packed
    at_gram = at_weight + shard
    at_count = at_gram + head
    for k in range(RING):
        for b in range(blocks):
            g = split_t[k * shard + b * size:k * shard + (b + 1) * size, :]
            gram = nt_dot(g, g)
            stats[k, b * packed:b * packed + size, :] = gram[:, 0:head].astype(BF16)
            stats[k, b * packed + size:(b + 1) * packed, 0:size - head] = gram[head:, head:].astype(BF16)
        weight = jnp.dot(split_t[k * shard:(k + 1) * shard, :], stacked, preferred_element_type=F32)
        stats[k, at_weight:at_gram, :] = weight.astype(BF16)
        stats[k, at_gram:at_count, :] = gram_in.astype(BF16)
        stats[k, at_count:, :] = counts.astype(BF16)
    stat = [
        send(
            stats.at[lax.rem(z + r, RING)], stats_in.at[r - 1],
            stats_send.at[r - 1], stats_recv.at[r - 1], along_z(r),
        )
        for r in (1, 2, 3)
    ]

    for copy in ins_z:
        copy.wait_recv()
    own_span = pl.ds(pl.multiple_of(x * span, 16), span)
    ins_x = [
        send(in_rows.at[own_span], in_rows.at[own_span], in_send.at[3 + r], in_recv.at[3 + r], along_x(r))
        for r in (1, 2, 3)
    ]

    total = part[0:rows, :]
    for r in (1, 2, 3):
        partials[r - 1].wait_recv()
        total = total + partial_in[r - 1].astype(F32)
    branch[...] = total.astype(BF16)
    branches = send(branch, branch_in, relay_send.at[1], relay_recv.at[1], before)

    for copy in stat:
        copy.wait_recv()
    total = stats[z].astype(F32)
    for r in (1, 2, 3):
        total = total + stats_in[r - 1].astype(F32)
    count = jnp.sum(total[at_count:, :], axis=0, keepdims=True)
    in_factor[...] = total[at_gram:at_count, :] / count
    count = count[:, 0:1]
    for b in range(blocks):
        full = total[b * packed:b * packed + size, :] / count
        corner = total[b * packed + size:(b + 1) * packed, 0:size - head] / count
        out_factor[b, :, 0:head] = full
        out_factor[b, head:, head:] = corner
        out_factor[b, 0:head, head:] = full[head:, :].T
        weight = total[at_weight + b * size:at_weight + (b + 1) * size, :] / jnp.sqrt(count)
        left = jnp.dot(out_inverse[b], weight, precision=lax.Precision.HIGHEST, preferred_element_type=F32)
        precond[b * size:(b + 1) * size, :] = jnp.dot(
            left, in_inverse[...], precision=lax.Precision.HIGHEST, preferred_element_type=F32
        )

    for copy in ins_x:
        copy.wait_recv()
    relay.wait_recv()
    branches.wait_recv()
    tile = 512
    scale = jnp.where(section == sections - 1, 0.0, 1.0).astype(F32)
    for c in range(width // tile):
        columns = slice(c * tile, (c + 1) * tile)
        sums = relayed[:, columns].astype(F32) + nt_dot(branch_in[...], in_rows[columns, :])
        passed[:, columns] = (sums * scale).astype(BF16)

    for copy in outs + vals + [ins, relay, branches] + ins_z + ins_x + partials + stat + [splits[r] for r in (1, 2, 3)]:
        copy.wait_send()


def local(upstream, inputs, in_proj, out_proj, in_inverse, out_inverse, lengths):
    _, batches, slots, width = upstream.shape
    rows = batches * slots
    head = inputs.shape[3]
    shard = in_proj.shape[1]
    blocks, size = out_inverse.shape[1:3]
    span = RING * shard
    stat_rows = blocks * (2 * size - head) + shard + head + 16
    vmem = pl.BlockSpec(memory_space=pltpu.VMEM)
    dma = pltpu.SemaphoreType.DMA
    outs = pl.pallas_call(
        kernel,
        out_shape=(
            jax.ShapeDtypeStruct((rows, width), BF16),
            jax.ShapeDtypeStruct((shard, head), F32),
            jax.ShapeDtypeStruct((head, head), F32),
            jax.ShapeDtypeStruct((blocks, size, size), F32),
        ),
        in_specs=[pl.BlockSpec(memory_space=pltpu.SMEM)] + [vmem] * 6,
        out_specs=(vmem,) * 4,
        scratch_shapes=[
            pltpu.VMEM((rows, width), BF16),
            pltpu.VMEM((RING * rows, span), BF16),
            pltpu.VMEM((span, RING * rows), BF16),
            pltpu.VMEM((rows, width), BF16),
            pltpu.VMEM((RING, rows + 16, head), BF16),
            pltpu.VMEM((span, head), BF16),
            pltpu.VMEM((width, head), BF16),
            pltpu.VMEM((RING * rows, head), BF16),
            pltpu.VMEM((RING - 1, rows, head), BF16),
            pltpu.VMEM((rows, head), BF16),
            pltpu.VMEM((rows, head), BF16),
            pltpu.VMEM((RING, stat_rows, head), BF16),
            pltpu.VMEM((RING - 1, stat_rows, head), BF16),
            dma((3,)), dma((3,)), dma((3,)), dma((3,)), dma((3,)), dma((3,)),
            dma((2,)), dma((2,)), dma((7,)), dma((7,)), dma((3,)), dma((3,)), dma((3,)), dma((3,)),
        ],
        compiler_params=pltpu.CompilerParams(
            collective_id=0, has_side_effects=True, vmem_limit_bytes=48 * 1024 * 1024
        ),
    )(
        lengths.reshape(batches),
        upstream.reshape(rows, width),
        inputs.reshape(rows, head),
        in_proj[0],
        out_proj[0],
        in_inverse[0],
        out_inverse[0],
    )
    passed, precond, in_factor, out_factor = outs
    return (passed.reshape(upstream.shape), precond[None], in_factor[None], out_factor[None])


def solution(mesh):
    in_specs = (
        P("section", None, "dp", None),
        P("section", None, "dp", None),
        P("section", "dp", None),
        P("section", "dp", None),
        P("section", None, None),
        P("section", "dp", None, None),
        P("section", "dp", None),
    )
    out_specs = (
        P("section", None, "dp", None),
        P("section", "dp", None),
        P("section", None, None),
        P("section", "dp", None, None),
    )
    return jax.shard_map(local, mesh=mesh, in_specs=in_specs, out_specs=out_specs, check_vma=False)
```

```python
import jax
import jax.numpy as jnp
from jax import lax
from jax.experimental import pallas as pl
from jax.experimental.pallas import tpu as pltpu
from jax.sharding import PartitionSpec as P

RING = 4
BF16 = jnp.bfloat16
F32 = jnp.float32
MESH = pl.DeviceIdType.MESH
VMEM_LIMIT = 56 * 1024 * 1024


def nt_dot(a, b):
    return lax.dot_general(a, b, (((1,), (1,)), ((), ())), preferred_element_type=F32)


def tn_dot(a, b):
    return lax.dot_general(a, b, (((0,), (0,)), ((), ())), preferred_element_type=F32)


def grid_of(shape):
    return lax.broadcasted_iota(jnp.int32, shape, 0), lax.broadcasted_iota(jnp.int32, shape, 1)


def pack_pair(first, second):
    row, column = grid_of(first.shape)
    return jnp.where(column > row, first, second)


def diagonal(matrix):
    row, column = grid_of(matrix.shape)
    return jnp.sum(jnp.where(column == row, matrix, 0.0), axis=0, keepdims=True)


def unpack_pair(packed, diagonal_row):
    row, column = grid_of(packed.shape)
    flipped = packed.T
    first = jnp.where(column > row, packed, jnp.where(column < row, flipped, diagonal_row))
    second = jnp.where(column > row, flipped, packed)
    return first, second


def kernel(
    lengths_hbm, upstream, inputs, in_proj, out_proj, in_inverse_hbm, out_inverse_hbm,
    passed_hbm, precond_hbm, in_factor_hbm, out_factor_hbm,
    passed, precond, in_factor, out_factor, lengths, raw, raw_values, in_inverse, out_inverse,
    sent, split, split_t, relayed, values, out_rows, in_rows, partial, partial_in, branch, branch_in,
    own_gram, gram_in, quarter, quarter_in, stats, half_in, stats_in,
    load, drain, split_send, split_recv, value_send, value_recv, out_send, out_recv,
    relay_send, relay_recv, in_send, in_recv, partial_send, partial_recv, gram_send, gram_recv,
    quarter_send, quarter_recv, stats_send, stats_recv,
):
    rows, width = upstream.shape
    slots = rows // lengths.shape[0]
    shard, head = in_proj.shape
    blocks, size, _ = out_inverse.shape
    span = RING * shard
    edge = size - head
    sections = lax.axis_size("section")
    dp = lax.axis_index("dp")
    section = lax.axis_index("section")
    x = lax.div(dp, RING)
    z = lax.rem(dp, RING)
    before = {"section": lax.rem(section + sections - 1, sections)}
    after = {"section": lax.rem(section + 1, sections)}

    def along_x(r):
        return {"dp": lax.rem(x + r, RING) * RING + z}

    def along_z(r):
        return {"dp": x * RING + lax.rem(z + r, RING)}

    started = []

    def send(src, dst, send_sem, recv_sem, device):
        copy = pltpu.make_async_remote_copy(
            src_ref=src, dst_ref=dst, send_sem=send_sem, recv_sem=recv_sem, device_id=device, device_id_type=MESH
        )
        copy.start()
        started.append(copy)
        return copy

    def fetch(src, dst, sem):
        copy = pltpu.make_async_copy(src, dst, sem)
        copy.start()
        return copy

    def span_at(r):
        return pl.ds(pl.multiple_of(lax.rem(x + r, RING) * span, head), span)

    def shard_at(device_x, device_z):
        return pl.ds(pl.multiple_of((device_x * RING + device_z) * shard, 16), shard)

    def half_shard(device_x, device_z, which):
        return pl.ds(pl.multiple_of((device_x * RING + device_z) * shard + which * (shard // 2), 16), shard // 2)

    barrier = pltpu.get_barrier_semaphore()
    for device in [along_x(r) for r in (1, 2, 3)] + [along_z(r) for r in (1, 2, 3)] + [before, after]:
        pl.semaphore_signal(barrier, inc=1, device_id=device, device_id_type=MESH)

    own_out = pl.ds(pl.multiple_of(z * shard, 16), shard)
    loads = [fetch(lengths_hbm, lengths, load.at[0]), fetch(inputs, raw_values, load.at[1])]
    spans = {r: fetch(upstream.at[:, span_at(r)], raw.at[r], load.at[2 + r]) for r in (2, 1, 3, 0)}
    own_rows = fetch(out_proj, out_rows.at[own_out], load.at[6])
    inverses = [fetch(in_inverse_hbm, in_inverse, load.at[7]), fetch(out_inverse_hbm, out_inverse, load.at[8])]

    for copy in loads:
        copy.wait()
    position = lax.broadcasted_iota(jnp.int32, (rows, 1), 0)
    batch = lax.div(position, slots)
    limit = jnp.where(batch == 0, lengths[0], jnp.where(batch == 1, lengths[1], lengths[2]))
    keep = (lax.rem(position, slots) < limit).astype(F32)
    keep = jnp.broadcast_to(keep, (rows, head)).astype(BF16)
    counted = (lengths[0] + lengths[1] + lengths[2]).astype(F32)
    values[0, 0:rows, :] = raw_values[...] * keep
    values[0, rows:, :] = jnp.full((16, head), counted, F32).astype(BF16)
    shared = (RING + 1) * head
    pair = 2 * head
    tile_at = [3 * p for p in range(RING + 1)] + [3 * k + 1 + j for k in range(RING) for j in range(2)]

    def mask(r):
        spans[r].wait()
        for p, tile in enumerate(tile_at):
            masked = raw[r, :, tile * head:(tile + 1) * head] * keep
            sent[r, :, p * head:(p + 1) * head] = masked
            if r == 0:
                split[0:rows, p * head:(p + 1) * head] = masked

    mask(2)

    pl.semaphore_wait(barrier, 8)

    out_a = send(out_proj, out_rows.at[own_out], out_send.at[0], out_recv.at[0], along_z(1))
    out_b = send(out_proj, out_rows.at[own_out], out_send.at[1], out_recv.at[1], along_z(3))
    own_in = shard_at(x, z)
    in_first = send(in_proj, in_rows.at[own_in], in_send.at[0], in_recv.at[0], before)

    vals = [send(values.at[0], values.at[r], value_send.at[r - 1], value_recv.at[r - 1], along_x(r)) for r in (1, 2, 3)]

    def pair_at(step):
        return pl.ds(pl.multiple_of(shared + lax.rem(z + step, RING) * pair, head), pair)

    def scatter(step, r):
        where = pl.ds(0, shared) if step is None else pair_at(step)
        at = 0 if step is None else step + 1
        return send(
            sent.at[r, :, where], split.at[pl.ds(r * rows, rows), where],
            split_send.at[at, r - 1], split_recv.at[at, r - 1], along_x(r),
        )

    splits = {}
    for r in (2, 1, 3):
        if r != 2:
            mask(r)
        splits[None, r] = scatter(None, r)
    for r in (2, 1, 3):
        splits[2, r] = scatter(2, r)
    mask(0)
    for step in (1, 3, 0):
        for r in (2, 1, 3):
            splits[step, r] = scatter(step, r)

    def arrived(step):
        for r in (1, 3, 2):
            splits[step, r].wait_recv()

    cuts = ((0, shared), (shared, 2 * pair), (shared + 2 * pair, 2 * pair))
    relays = {}

    def relay(*pieces):
        for piece in pieces:
            r, cut = (0, 3, 1, 2)[piece // 3], piece % 3
            where = pl.ds(*cuts[cut])
            relays[r, cut] = send(
                sent.at[r, :, where], relayed.at[r, :, where], relay_send.at[piece], relay_recv.at[piece], before
            )

    in_first.wait_recv()
    in_a = send(in_rows.at[own_in], in_rows.at[own_in], in_send.at[1], in_recv.at[1], along_z(1))
    in_b = send(in_rows.at[own_in], in_rows.at[own_in], in_send.at[2], in_recv.at[2], along_z(3))
    left, right = lax.rem(z + 3, RING), lax.rem(z + 1, RING)
    half = shard // 2
    low = pl.ds(pl.multiple_of(left * shard, 16), half)
    high = pl.ds(pl.multiple_of(right * shard + half, 16), half)
    out_a.wait_recv()
    out_c = send(out_rows.at[low], out_rows.at[low], out_send.at[2], out_recv.at[2], along_z(1))
    out_b.wait_recv()
    out_d = send(out_rows.at[high], out_rows.at[high], out_send.at[3], out_recv.at[3], along_z(3))

    for copy in vals:
        copy.wait_recv()
    stacked = jnp.concatenate([values[r, 0:rows, :] for r in range(RING)], axis=0)
    quart = head // RING
    own_gram[...] = tn_dot(stacked, stacked).astype(BF16)
    gram_in[0, 0:quart, :] = own_gram[pl.ds(pl.multiple_of(x * quart, 16), quart), :]
    count_row = lax.broadcasted_iota(jnp.int32, (16, head), 0)
    counts = jnp.zeros((16, head), F32)
    for r in range(RING):
        counts = jnp.where(count_row == r, values[r, rows:, :].astype(F32), counts)
    gram_in[0, quart:, :] = counts.astype(BF16)
    grams = [send(gram_in.at[0], gram_in.at[r], gram_send.at[r - 1], gram_recv.at[r - 1], along_z(r)) for r in (1, 2, 3)]

    in_a.wait_recv()
    low_in = half_shard(x, left, 0)
    in_c = send(in_rows.at[low_in], in_rows.at[low_in], in_send.at[3], in_recv.at[3], along_z(1))
    in_b.wait_recv()
    high_in = half_shard(x, right, 1)
    in_d = send(in_rows.at[high_in], in_rows.at[high_in], in_send.at[4], in_recv.at[4], along_z(3))

    for copy in grams:
        copy.wait_recv()
    total = gram_in[0].astype(F32)
    for r in (1, 2, 3):
        total = total + gram_in[r].astype(F32)
    count = jnp.sum(total[quart:, :], axis=0, keepdims=True)
    quarter[...] = total[0:quart, :] / count
    count = count[:, 0:1]
    quarters = [
        send(quarter, quarter_in.at[r - 1], quarter_send.at[r - 1], quarter_recv.at[r - 1], along_x(r)) for r in (1, 2, 3)
    ]

    arrived(None)
    for p in range(RING + 1):
        split_t[3 * p * head:(3 * p + 1) * head, :] = split[:, p * head:(p + 1) * head].T

    def turn(step):
        first = (3 * lax.rem(z + step, RING) + 1) * head
        split_t[pl.ds(pl.multiple_of(first, head), pair), :] = split[:, pair_at(step)].T

    at_edge = head
    at_corner = at_edge + blocks * edge
    at_diagonal = at_corner + edge
    at_weight = at_diagonal + 16
    diagonal_row = lax.broadcasted_iota(jnp.int32, (16, head), 0)

    def statistics(r):
        owner = lax.rem(z + r, RING) * shard
        grams = []
        for b in range(blocks):
            g = split_t[pl.ds(pl.multiple_of(owner + b * size, 16), size), :]
            grams.append(nt_dot(g, g))
            stats[r, at_edge + b * edge:at_edge + (b + 1) * edge, :] = grams[b][head:, 0:head].astype(BF16)
        stats[r, 0:head, :] = pack_pair(grams[0][0:head, 0:head], grams[1][0:head, 0:head]).astype(BF16)
        corner = pack_pair(grams[0][head:, head:], grams[1][head:, head:])
        stats[r, at_corner:at_diagonal, 0:edge] = corner.astype(BF16)
        first = diagonal(grams[0][0:head, 0:head])
        stats[r, at_diagonal:at_weight, :] = jnp.where(diagonal_row == 0, first, 0.0).astype(BF16)
        second = diagonal(grams[0][head:, head:])
        stats[r, at_diagonal:at_weight, 0:edge] = jnp.where(
            diagonal_row[:, 0:edge] == 0, first[:, 0:edge], jnp.where(diagonal_row[:, 0:edge] == 1, second, 0.0)
        ).astype(BF16)
        weight = jnp.dot(
            split_t[pl.ds(pl.multiple_of(owner, 16), shard), :], stacked, preferred_element_type=F32
        )
        stats[r, at_weight:, :] = weight.astype(BF16)

    stat_rows = stats.shape[1]
    cut = stat_rows // 2
    top, bottom = pl.ds(0, cut), pl.ds(cut, cut)
    arrived(2)
    turn(2)
    statistics(2)
    half_a = send(stats.at[2, top], half_in.at[0], stats_send.at[0], stats_recv.at[0], along_z(1))
    half_b = send(stats.at[2, bottom], half_in.at[1], stats_send.at[1], stats_recv.at[1], along_z(3))
    arrived(1)
    turn(1)
    statistics(1)
    near_b = send(stats.at[1, bottom], stats_in.at[0, bottom], stats_send.at[2], stats_recv.at[2], along_z(1))
    arrived(3)
    turn(3)
    statistics(3)
    near_a = send(stats.at[3, top], stats_in.at[1, top], stats_send.at[3], stats_recv.at[3], along_z(3))
    half_a.wait_recv()
    stats[1, top, :] = (stats[1, top, :].astype(F32) + half_in[0].astype(F32)).astype(BF16)
    far_a = send(stats.at[1, top], stats_in.at[0, top], stats_send.at[4], stats_recv.at[4], along_z(1))
    half_b.wait_recv()
    stats[3, bottom, :] = (stats[3, bottom, :].astype(F32) + half_in[1].astype(F32)).astype(BF16)
    far_b = send(stats.at[3, bottom], stats_in.at[1, bottom], stats_send.at[5], stats_recv.at[5], along_z(3))

    arrived(0)
    own_rows.wait()
    out_c.wait_recv()
    out_d.wait_recv()
    ordered = [out_rows[3 * p * head:(3 * p + 1) * head, :] for p in range(RING + 1)]
    ordered += [out_rows[(3 * k + 1) * head:(3 * k + 3) * head, :] for k in range(RING)]
    part = jnp.dot(split[...], jnp.concatenate(ordered, axis=0), preferred_element_type=F32)
    partial[...] = part.astype(BF16)
    partials = [
        send(
            partial.at[pl.ds(r * rows, rows)], partial_in.at[r - 1],
            partial_send.at[r - 1], partial_recv.at[r - 1], along_x(RING - r),
        )
        for r in (1, 2, 3)
    ]

    in_c.wait_recv()
    in_d.wait_recv()
    own_span = pl.ds(pl.multiple_of(x * span, 16), span)
    in_x = [
        send(in_rows.at[own_span], in_rows.at[own_span], in_send.at[4 + r], in_recv.at[4 + r], along_x(r))
        for r in (1, 3, 2)
    ]

    turn(0)
    statistics(0)
    total = part[0:rows, :]
    for r in (1, 2, 3):
        partials[r - 1].wait_recv()
        total = total + partial_in[r - 1].astype(F32)
    branch[...] = total.astype(BF16)
    branches = send(branch, branch_in, relay_send.at[12], relay_recv.at[12], before)
    relay(*range(12))

    in_factor[pl.ds(pl.multiple_of(x * quart, 16), quart), :] = quarter[...]
    for r in (1, 2, 3):
        quarters[r - 1].wait_recv()
        source = lax.rem(x + RING - r, RING)
        in_factor[pl.ds(pl.multiple_of(source * quart, 16), quart), :] = quarter_in[r - 1]
    drained = [fetch(in_factor, in_factor_hbm, drain.at[0])]

    for copy in (near_a, near_b, far_a, far_b):
        copy.wait_recv()
    for copy in inverses:
        copy.wait()
    total = stats[0].astype(F32) + stats_in[0].astype(F32) + stats_in[1].astype(F32)
    heads = unpack_pair(total[0:head, :], total[at_diagonal:at_diagonal + 1, :])
    corners = unpack_pair(total[at_corner:at_diagonal, 0:edge], total[at_diagonal + 1:at_diagonal + 2, 0:edge])
    for b in range(blocks):
        side = total[at_edge + b * edge:at_edge + (b + 1) * edge, :] / count
        out_factor[b, 0:head, 0:head] = heads[b] / count
        out_factor[b, head:, 0:head] = side
        out_factor[b, 0:head, head:] = side.T
        out_factor[b, head:, head:] = corners[b] / count
        weight = total[at_weight + b * size:at_weight + (b + 1) * size, :] / jnp.sqrt(count)
        left_product = jnp.dot(out_inverse[b], weight, precision=lax.Precision.HIGHEST, preferred_element_type=F32)
        precond[b * size:(b + 1) * size, :] = jnp.dot(
            left_product, in_inverse[...], precision=lax.Precision.HIGHEST, preferred_element_type=F32
        )

    drained += [fetch(precond, precond_hbm, drain.at[1]), fetch(out_factor, out_factor_hbm, drain.at[2])]

    branches.wait_recv()
    scale = jnp.where(section == sections - 1, 0.0, 1.0).astype(F32)
    for copy, r in zip([None] + in_x, (0, 3, 1, 2)):
        if copy is not None:
            copy.wait_recv()
        first = lax.rem(x + r, RING) * span
        for cut, (start, extent) in enumerate(cuts):
            relays[r, cut].wait_recv()
            step = head if cut == 0 else pair
            for at in range(start, start + extent, step):
                columns = pl.ds(pl.multiple_of(first + tile_at[at // head] * head, head), step)
                sums = relayed[r, :, at:at + step].astype(F32) + nt_dot(branch_in[...], in_rows[columns, :])
                passed[:, columns] = (sums * scale).astype(BF16)
        drained.append(fetch(passed.at[:, span_at(r)], passed_hbm.at[:, span_at(r)], drain.at[3 + r]))

    for copy in started:
        copy.wait_send()
    for copy in drained:
        copy.wait()


def store(*refs):
    sources, targets, held, arrive, leave = refs[:4], refs[4:8], refs[8:12], refs[12], refs[13]
    width = sources[0].shape[1]
    piece = width // 4
    views = [lambda ref, i=i: ref.at[:, pl.ds(i * piece, piece)] for i in range(4)]
    parts = [(view(sources[0]), view(held[0]), view(targets[0])) for view in views]
    parts += list(zip(sources[1:], held[1:], targets[1:]))
    loads = [pltpu.make_async_copy(part[0], part[1], arrive.at[i]) for i, part in enumerate(parts)]
    stores = [pltpu.make_async_copy(part[1], part[2], leave.at[i]) for i, part in enumerate(parts)]
    for copy in loads:
        copy.start()
    for load, copy in zip(loads, stores):
        load.wait()
        copy.start()
    for copy in stores:
        copy.wait()


def local(upstream, inputs, in_proj, out_proj, in_inverse, out_inverse, lengths):
    _, batches, slots, width = upstream.shape
    rows = batches * slots
    head = inputs.shape[3]
    shard = in_proj.shape[1]
    blocks, size = out_inverse.shape[1:3]
    span = RING * shard
    edge = size - head
    stat_rows = head + blocks * edge + edge + 16 + shard
    hbm = pl.BlockSpec(memory_space=pltpu.HBM)
    dma = pltpu.SemaphoreType.DMA
    shapes = (
        jax.ShapeDtypeStruct((rows, width), BF16),
        jax.ShapeDtypeStruct((shard, head), F32),
        jax.ShapeDtypeStruct((head, head), F32),
        jax.ShapeDtypeStruct((blocks, size, size), F32),
    )
    outs = pl.pallas_call(
        kernel,
        out_shape=shapes,
        in_specs=[hbm] * 7,
        out_specs=(hbm,) * 4,
        scratch_shapes=[
            pltpu.VMEM((rows, width), BF16),
            pltpu.VMEM((shard, head), F32),
            pltpu.VMEM((head, head), F32),
            pltpu.VMEM((blocks, size, size), F32),
            pltpu.SMEM((batches,), jnp.int32),
            pltpu.VMEM((RING, rows, span), BF16),
            pltpu.VMEM((rows, head), BF16),
            pltpu.VMEM((head, head), F32),
            pltpu.VMEM((blocks, size, size), F32),
            pltpu.VMEM((RING, rows, span), BF16),
            pltpu.VMEM((RING * rows, span), BF16),
            pltpu.VMEM((span, RING * rows), BF16),
            pltpu.VMEM((RING, rows, span), BF16),
            pltpu.VMEM((RING, rows + 16, head), BF16),
            pltpu.VMEM((span, head), BF16),
            pltpu.VMEM((width, head), BF16),
            pltpu.VMEM((RING * rows, head), BF16),
            pltpu.VMEM((RING - 1, rows, head), BF16),
            pltpu.VMEM((rows, head), BF16),
            pltpu.VMEM((rows, head), BF16),
            pltpu.VMEM((head, head), BF16),
            pltpu.VMEM((RING, head // RING + 16, head), BF16),
            pltpu.VMEM((head // RING, head), F32),
            pltpu.VMEM((RING - 1, head // RING, head), F32),
            pltpu.VMEM((RING, stat_rows, head), BF16),
            pltpu.VMEM((2, stat_rows // 2, head), BF16),
            pltpu.VMEM((2, stat_rows, head), BF16),
            dma((9,)), dma((7,)), dma((5, 3)), dma((5, 3)), dma((3,)), dma((3,)), dma((4,)), dma((4,)),
            dma((13,)), dma((13,)), dma((8,)), dma((8,)), dma((3,)), dma((3,)), dma((3,)), dma((3,)),
            dma((3,)), dma((3,)), dma((6,)), dma((6,)),
        ],
        compiler_params=pltpu.CompilerParams(
            collective_id=0, has_side_effects=True, vmem_limit_bytes=VMEM_LIMIT
        ),
    )(
        lengths.reshape(batches),
        upstream.reshape(rows, width),
        inputs.reshape(rows, head),
        in_proj[0],
        out_proj[0],
        in_inverse[0],
        out_inverse[0],
    )
    passed, precond, in_factor, out_factor = pl.pallas_call(
        store,
        out_shape=shapes,
        in_specs=[hbm] * 4,
        out_specs=(hbm,) * 4,
        scratch_shapes=[pltpu.VMEM(shape.shape, shape.dtype) for shape in shapes] + [dma((7,)), dma((7,))],
        compiler_params=pltpu.CompilerParams(vmem_limit_bytes=VMEM_LIMIT),
    )(*outs)
    return (passed.reshape(upstream.shape), precond[None], in_factor[None], out_factor[None])


def solution(mesh):
    in_specs = (
        P("section", None, "dp", None),
        P("section", None, "dp", None),
        P("section", "dp", None),
        P("section", "dp", None),
        P("section", None, None),
        P("section", "dp", None, None),
        P("section", "dp", None),
    )
    out_specs = (
        P("section", None, "dp", None),
        P("section", "dp", None),
        P("section", None, None),
        P("section", "dp", None, None),
    )
    return jax.shard_map(local, mesh=mesh, in_specs=in_specs, out_specs=out_specs, check_vma=False)
```

```python
import jax
import jax.numpy as jnp
from jax import lax
from jax.experimental import pallas as pl
from jax.experimental.pallas import tpu as pltpu
from jax.sharding import PartitionSpec as P

RING = 4
BF16 = jnp.bfloat16
F32 = jnp.float32
MESH = pl.DeviceIdType.MESH
VMEM_LIMIT = 56 * 1024 * 1024


def nt_dot(a, b):
    return lax.dot_general(a, b, (((1,), (1,)), ((), ())), preferred_element_type=F32)


def tn_dot(a, b):
    return lax.dot_general(a, b, (((0,), (0,)), ((), ())), preferred_element_type=F32)


def grid_of(shape):
    return lax.broadcasted_iota(jnp.int32, shape, 0), lax.broadcasted_iota(jnp.int32, shape, 1)


def pack_pair(first, second):
    row, column = grid_of(first.shape)
    return jnp.where(column > row, first, second)


def diagonal(matrix):
    row, column = grid_of(matrix.shape)
    return jnp.sum(jnp.where(column == row, matrix, 0.0), axis=0, keepdims=True)


def unpack_pair(packed, diagonal_row):
    row, column = grid_of(packed.shape)
    flipped = packed.T
    first = jnp.where(column > row, packed, jnp.where(column < row, flipped, diagonal_row))
    second = jnp.where(column > row, flipped, packed)
    return first, second


def kernel(
    lengths_hbm, upstream, inputs, in_proj, out_proj, in_inverse_hbm, out_inverse_hbm,
    passed_hbm, precond_hbm, in_factor_hbm, out_factor_hbm,
    passed, precond, in_factor, out_factor, lengths, raw, raw_values, raw_proj, in_inverse, out_inverse,
    sent, split, split_t, relayed, values, out_rows, in_rows, partial, partial_in, branch, branch_in,
    own_gram, gram_in, quarter, quarter_in, stats, half_in, stats_in,
    load, drain, split_send, split_recv, value_send, value_recv, out_send, out_recv,
    relay_send, relay_recv, in_send, in_recv, partial_send, partial_recv, gram_send, gram_recv,
    quarter_send, quarter_recv, stats_send, stats_recv,
):
    rows, width = upstream.shape
    slots = rows // lengths.shape[0]
    shard, head = in_proj.shape
    blocks, size, _ = out_inverse.shape
    span = RING * shard
    edge = size - head
    sections = lax.axis_size("section")
    dp = lax.axis_index("dp")
    section = lax.axis_index("section")
    x = lax.div(dp, RING)
    z = lax.rem(dp, RING)
    before = {"section": lax.rem(section + sections - 1, sections)}
    after = {"section": lax.rem(section + 1, sections)}

    def along_x(r):
        return {"dp": lax.rem(x + r, RING) * RING + z}

    def along_z(r):
        return {"dp": x * RING + lax.rem(z + r, RING)}

    started = []

    def send(src, dst, send_sem, recv_sem, device):
        copy = pltpu.make_async_remote_copy(
            src_ref=src, dst_ref=dst, send_sem=send_sem, recv_sem=recv_sem, device_id=device, device_id_type=MESH
        )
        copy.start()
        started.append(copy)
        return copy

    def fetch(src, dst, sem):
        copy = pltpu.make_async_copy(src, dst, sem)
        copy.start()
        return copy

    def span_at(r):
        return pl.ds(pl.multiple_of(lax.rem(x + r, RING) * span, head), span)

    def shard_at(device_x, device_z):
        return pl.ds(pl.multiple_of((device_x * RING + device_z) * shard, 16), shard)

    def half_shard(device_x, device_z, which):
        return pl.ds(pl.multiple_of((device_x * RING + device_z) * shard + which * (shard // 2), 16), shard // 2)

    barrier = pltpu.get_barrier_semaphore()
    for device in [along_x(r) for r in (1, 2, 3)] + [along_z(r) for r in (1, 2, 3)] + [before, after]:
        pl.semaphore_signal(barrier, inc=1, device_id=device, device_id_type=MESH)

    own_out = pl.ds(pl.multiple_of(z * shard, 16), shard)
    own_rows = fetch(out_proj, out_rows.at[own_out], load.at[6])
    own_proj = fetch(in_proj, raw_proj, load.at[9])
    loads = [fetch(lengths_hbm, lengths, load.at[0]), fetch(inputs, raw_values, load.at[1])]
    spans = {r: fetch(upstream.at[:, span_at(r)], raw.at[r], load.at[2 + r]) for r in (2, 1, 3, 0)}
    inverses = [fetch(in_inverse_hbm, in_inverse, load.at[7]), fetch(out_inverse_hbm, out_inverse, load.at[8])]

    for copy in loads:
        copy.wait()
    position = lax.broadcasted_iota(jnp.int32, (rows, 1), 0)
    batch = lax.div(position, slots)
    limit = jnp.where(batch == 0, lengths[0], jnp.where(batch == 1, lengths[1], lengths[2]))
    keep = (lax.rem(position, slots) < limit).astype(F32)
    keep = jnp.broadcast_to(keep, (rows, head)).astype(BF16)
    counted = (lengths[0] + lengths[1] + lengths[2]).astype(F32)
    values[0, 0:rows, :] = raw_values[...] * keep
    values[0, rows:, :] = jnp.full((16, head), counted, F32).astype(BF16)
    shared = (RING + 1) * head
    pair = 2 * head
    tile_at = [3 * p for p in range(RING + 1)] + [3 * k + 1 + j for k in range(RING) for j in range(2)]

    def mask(r):
        spans[r].wait()
        for p, tile in enumerate(tile_at):
            masked = raw[r, :, tile * head:(tile + 1) * head] * keep
            sent[r, :, p * head:(p + 1) * head] = masked
            if r == 0:
                split[0:rows, p * head:(p + 1) * head] = masked

    mask(2)

    pl.semaphore_wait(barrier, 8)

    own_rows.wait()
    own_proj.wait()
    out_a = send(out_rows.at[own_out], out_rows.at[own_out], out_send.at[0], out_recv.at[0], along_z(1))
    out_b = send(out_rows.at[own_out], out_rows.at[own_out], out_send.at[1], out_recv.at[1], along_z(3))
    own_in = shard_at(x, z)
    in_first = send(raw_proj, in_rows.at[own_in], in_send.at[0], in_recv.at[0], before)

    vals = [send(values.at[0], values.at[r], value_send.at[r - 1], value_recv.at[r - 1], along_x(r)) for r in (1, 2, 3)]

    def pair_at(step):
        return pl.ds(pl.multiple_of(shared + lax.rem(z + step, RING) * pair, head), pair)

    def scatter(step, r):
        where = pl.ds(0, shared) if step is None else pair_at(step)
        at = 0 if step is None else step + 1
        return send(
            sent.at[r, :, where], split.at[pl.ds(r * rows, rows), where],
            split_send.at[at, r - 1], split_recv.at[at, r - 1], along_x(r),
        )

    splits = {}
    for r in (2, 1, 3):
        if r != 2:
            mask(r)
        splits[None, r] = scatter(None, r)
    for r in (2, 1, 3):
        splits[2, r] = scatter(2, r)
    mask(0)
    for step in (1, 3, 0):
        for r in (2, 1, 3):
            splits[step, r] = scatter(step, r)

    def arrived(step):
        for r in (1, 3, 2):
            splits[step, r].wait_recv()

    cuts = ((0, shared), (shared, 2 * pair), (shared + 2 * pair, 2 * pair))
    relays = {}

    def relay(*pieces):
        for piece in pieces:
            r, cut = (0, 3, 1, 2)[piece // 3], piece % 3
            where = pl.ds(*cuts[cut])
            relays[r, cut] = send(
                sent.at[r, :, where], relayed.at[r, :, where], relay_send.at[piece], relay_recv.at[piece], before
            )

    in_first.wait_recv()
    in_a = send(in_rows.at[own_in], in_rows.at[own_in], in_send.at[1], in_recv.at[1], along_z(1))
    in_b = send(in_rows.at[own_in], in_rows.at[own_in], in_send.at[2], in_recv.at[2], along_z(3))
    left, right = lax.rem(z + 3, RING), lax.rem(z + 1, RING)
    half = shard // 2
    low = pl.ds(pl.multiple_of(left * shard, 16), half)
    high = pl.ds(pl.multiple_of(right * shard + half, 16), half)
    out_a.wait_recv()
    out_c = send(out_rows.at[low], out_rows.at[low], out_send.at[2], out_recv.at[2], along_z(1))
    out_b.wait_recv()
    out_d = send(out_rows.at[high], out_rows.at[high], out_send.at[3], out_recv.at[3], along_z(3))

    for copy in vals:
        copy.wait_recv()
    stacked = jnp.concatenate([values[r, 0:rows, :] for r in range(RING)], axis=0)
    quart = head // RING
    own_gram[...] = tn_dot(stacked, stacked).astype(BF16)
    gram_in[0, 0:quart, :] = own_gram[pl.ds(pl.multiple_of(x * quart, 16), quart), :]
    count_row = lax.broadcasted_iota(jnp.int32, (16, head), 0)
    counts = jnp.zeros((16, head), F32)
    for r in range(RING):
        counts = jnp.where(count_row == r, values[r, rows:, :].astype(F32), counts)
    gram_in[0, quart:, :] = counts.astype(BF16)
    grams = [send(gram_in.at[0], gram_in.at[r], gram_send.at[r - 1], gram_recv.at[r - 1], along_z(r)) for r in (1, 2, 3)]

    in_a.wait_recv()
    low_in = half_shard(x, left, 0)
    in_c = send(in_rows.at[low_in], in_rows.at[low_in], in_send.at[3], in_recv.at[3], along_z(1))
    in_b.wait_recv()
    high_in = half_shard(x, right, 1)
    in_d = send(in_rows.at[high_in], in_rows.at[high_in], in_send.at[4], in_recv.at[4], along_z(3))

    for copy in grams:
        copy.wait_recv()
    total = gram_in[0].astype(F32)
    for r in (1, 2, 3):
        total = total + gram_in[r].astype(F32)
    count = jnp.sum(total[quart:, :], axis=0, keepdims=True)
    quarter[...] = total[0:quart, :] / count
    count = count[:, 0:1]
    quarters = [
        send(quarter, quarter_in.at[r - 1], quarter_send.at[r - 1], quarter_recv.at[r - 1], along_x(r)) for r in (1, 2, 3)
    ]

    arrived(None)
    for p in range(RING + 1):
        split_t[3 * p * head:(3 * p + 1) * head, :] = split[:, p * head:(p + 1) * head].T

    def turn(step):
        first = (3 * lax.rem(z + step, RING) + 1) * head
        split_t[pl.ds(pl.multiple_of(first, head), pair), :] = split[:, pair_at(step)].T

    at_edge = head
    at_corner = at_edge + blocks * edge
    at_diagonal = at_corner + edge
    at_weight = at_diagonal + 16
    diagonal_row = lax.broadcasted_iota(jnp.int32, (16, head), 0)

    def statistics(r):
        owner = lax.rem(z + r, RING) * shard
        grams = []
        for b in range(blocks):
            g = split_t[pl.ds(pl.multiple_of(owner + b * size, 16), size), :]
            grams.append(nt_dot(g, g))
            stats[r, at_edge + b * edge:at_edge + (b + 1) * edge, :] = grams[b][head:, 0:head].astype(BF16)
        stats[r, 0:head, :] = pack_pair(grams[0][0:head, 0:head], grams[1][0:head, 0:head]).astype(BF16)
        corner = pack_pair(grams[0][head:, head:], grams[1][head:, head:])
        stats[r, at_corner:at_diagonal, 0:edge] = corner.astype(BF16)
        first = diagonal(grams[0][0:head, 0:head])
        stats[r, at_diagonal:at_weight, :] = jnp.where(diagonal_row == 0, first, 0.0).astype(BF16)
        second = diagonal(grams[0][head:, head:])
        stats[r, at_diagonal:at_weight, 0:edge] = jnp.where(
            diagonal_row[:, 0:edge] == 0, first[:, 0:edge], jnp.where(diagonal_row[:, 0:edge] == 1, second, 0.0)
        ).astype(BF16)
        weight = jnp.dot(
            split_t[pl.ds(pl.multiple_of(owner, 16), shard), :], stacked, preferred_element_type=F32
        )
        stats[r, at_weight:, :] = weight.astype(BF16)

    stat_rows = stats.shape[1]
    cut = stat_rows // 2
    top, bottom = pl.ds(0, cut), pl.ds(cut, cut)
    arrived(2)
    turn(2)
    statistics(2)
    half_a = send(stats.at[2, top], half_in.at[0], stats_send.at[0], stats_recv.at[0], along_z(1))
    half_b = send(stats.at[2, bottom], half_in.at[1], stats_send.at[1], stats_recv.at[1], along_z(3))
    arrived(1)
    turn(1)
    statistics(1)
    near_b = send(stats.at[1, bottom], stats_in.at[0, bottom], stats_send.at[2], stats_recv.at[2], along_z(1))
    arrived(3)
    turn(3)
    statistics(3)
    near_a = send(stats.at[3, top], stats_in.at[1, top], stats_send.at[3], stats_recv.at[3], along_z(3))
    arrived(0)
    out_c.wait_recv()
    out_d.wait_recv()
    ordered = [out_rows[3 * p * head:(3 * p + 1) * head, :] for p in range(RING + 1)]
    ordered += [out_rows[(3 * k + 1) * head:(3 * k + 3) * head, :] for k in range(RING)]
    part = jnp.dot(split[...], jnp.concatenate(ordered, axis=0), preferred_element_type=F32)
    partial[...] = part
    partials = [
        send(
            partial.at[pl.ds(r * rows, rows)], partial_in.at[r - 1],
            partial_send.at[r - 1], partial_recv.at[r - 1], along_x(RING - r),
        )
        for r in (1, 2, 3)
    ]

    in_c.wait_recv()
    in_d.wait_recv()
    own_span = pl.ds(pl.multiple_of(x * span, 16), span)
    in_x = [
        send(in_rows.at[own_span], in_rows.at[own_span], in_send.at[4 + r], in_recv.at[4 + r], along_x(r))
        for r in (1, 3, 2)
    ]

    half_a.wait_recv()
    stats[1, top, :] = (stats[1, top, :].astype(F32) + half_in[0].astype(F32)).astype(BF16)
    far_a = send(stats.at[1, top], stats_in.at[0, top], stats_send.at[4], stats_recv.at[4], along_z(1))
    half_b.wait_recv()
    stats[3, bottom, :] = (stats[3, bottom, :].astype(F32) + half_in[1].astype(F32)).astype(BF16)
    far_b = send(stats.at[3, bottom], stats_in.at[1, bottom], stats_send.at[5], stats_recv.at[5], along_z(3))

    turn(0)
    statistics(0)
    total = part[0:rows, :]
    for r in (1, 2, 3):
        partials[r - 1].wait_recv()
        total = total + partial_in[r - 1]
    branch[...] = total.astype(BF16)
    branches = send(branch, branch_in, relay_send.at[12], relay_recv.at[12], before)
    near_a.wait_recv()
    near_b.wait_recv()
    relay(*range(12))

    in_factor[pl.ds(pl.multiple_of(x * quart, 16), quart), :] = quarter[...]
    for r in (1, 2, 3):
        quarters[r - 1].wait_recv()
        source = lax.rem(x + RING - r, RING)
        in_factor[pl.ds(pl.multiple_of(source * quart, 16), quart), :] = quarter_in[r - 1]
    drained = [fetch(in_factor, in_factor_hbm, drain.at[0])]

    for copy in (far_a, far_b):
        copy.wait_recv()
    for copy in inverses:
        copy.wait()
    total = stats[0].astype(F32) + stats_in[0].astype(F32) + stats_in[1].astype(F32)
    heads = unpack_pair(total[0:head, :], total[at_diagonal:at_diagonal + 1, :])
    corners = unpack_pair(total[at_corner:at_diagonal, 0:edge], total[at_diagonal + 1:at_diagonal + 2, 0:edge])
    for b in range(blocks):
        side = total[at_edge + b * edge:at_edge + (b + 1) * edge, :] / count
        out_factor[b, 0:head, 0:head] = heads[b] / count
        out_factor[b, head:, 0:head] = side
        out_factor[b, 0:head, head:] = side.T
        out_factor[b, head:, head:] = corners[b] / count
        weight = total[at_weight + b * size:at_weight + (b + 1) * size, :] / jnp.sqrt(count)
        left_product = jnp.dot(out_inverse[b], weight, precision=lax.Precision.HIGHEST, preferred_element_type=F32)
        precond[b * size:(b + 1) * size, :] = jnp.dot(
            left_product, in_inverse[...], precision=lax.Precision.HIGHEST, preferred_element_type=F32
        )

    drained += [fetch(precond, precond_hbm, drain.at[1]), fetch(out_factor, out_factor_hbm, drain.at[2])]

    branches.wait_recv()
    scale = jnp.where(section == sections - 1, 0.0, 1.0).astype(F32)
    for copy, r in zip([None] + in_x, (0, 3, 1, 2)):
        if copy is not None:
            copy.wait_recv()
        first = lax.rem(x + r, RING) * span
        for cut, (start, extent) in enumerate(cuts):
            relays[r, cut].wait_recv()
            step = head if cut == 0 else pair
            for at in range(start, start + extent, step):
                columns = pl.ds(pl.multiple_of(first + tile_at[at // head] * head, head), step)
                sums = relayed[r, :, at:at + step].astype(F32) + nt_dot(branch_in[...], in_rows[columns, :])
                passed[:, columns] = (sums * scale).astype(BF16)
        drained.append(fetch(passed.at[:, span_at(r)], passed_hbm.at[:, span_at(r)], drain.at[3 + r]))

    for copy in started:
        copy.wait_send()
    for copy in drained:
        copy.wait()


def store(*refs):
    sources, targets, held, arrive, leave = refs[:4], refs[4:8], refs[8:12], refs[12], refs[13]
    width = sources[0].shape[1]
    piece = width // 4
    views = [lambda ref, i=i: ref.at[:, pl.ds(i * piece, piece)] for i in range(4)]
    parts = [(view(sources[0]), view(held[0]), view(targets[0])) for view in views]
    parts += list(zip(sources[1:], held[1:], targets[1:]))
    loads = [pltpu.make_async_copy(part[0], part[1], arrive.at[i]) for i, part in enumerate(parts)]
    stores = [pltpu.make_async_copy(part[1], part[2], leave.at[i]) for i, part in enumerate(parts)]
    for copy in loads:
        copy.start()
    for load, copy in zip(loads, stores):
        load.wait()
        copy.start()
    for copy in stores:
        copy.wait()


def local(upstream, inputs, in_proj, out_proj, in_inverse, out_inverse, lengths):
    _, batches, slots, width = upstream.shape
    rows = batches * slots
    head = inputs.shape[3]
    shard = in_proj.shape[1]
    blocks, size = out_inverse.shape[1:3]
    span = RING * shard
    edge = size - head
    stat_rows = head + blocks * edge + edge + 16 + shard
    hbm = pl.BlockSpec(memory_space=pltpu.HBM)
    dma = pltpu.SemaphoreType.DMA
    shapes = (
        jax.ShapeDtypeStruct((rows, width), BF16),
        jax.ShapeDtypeStruct((shard, head), F32),
        jax.ShapeDtypeStruct((head, head), F32),
        jax.ShapeDtypeStruct((blocks, size, size), F32),
    )
    outs = pl.pallas_call(
        kernel,
        out_shape=shapes,
        in_specs=[hbm] * 7,
        out_specs=(hbm,) * 4,
        scratch_shapes=[
            pltpu.VMEM((rows, width), BF16),
            pltpu.VMEM((shard, head), F32),
            pltpu.VMEM((head, head), F32),
            pltpu.VMEM((blocks, size, size), F32),
            pltpu.SMEM((batches,), jnp.int32),
            pltpu.VMEM((RING, rows, span), BF16),
            pltpu.VMEM((rows, head), BF16),
            pltpu.VMEM((shard, head), BF16),
            pltpu.VMEM((head, head), F32),
            pltpu.VMEM((blocks, size, size), F32),
            pltpu.VMEM((RING, rows, span), BF16),
            pltpu.VMEM((RING * rows, span), BF16),
            pltpu.VMEM((span, RING * rows), BF16),
            pltpu.VMEM((RING, rows, span), BF16),
            pltpu.VMEM((RING, rows + 16, head), BF16),
            pltpu.VMEM((span, head), BF16),
            pltpu.VMEM((width, head), BF16),
            pltpu.VMEM((RING * rows, head), F32),
            pltpu.VMEM((RING - 1, rows, head), F32),
            pltpu.VMEM((rows, head), BF16),
            pltpu.VMEM((rows, head), BF16),
            pltpu.VMEM((head, head), BF16),
            pltpu.VMEM((RING, head // RING + 16, head), BF16),
            pltpu.VMEM((head // RING, head), F32),
            pltpu.VMEM((RING - 1, head // RING, head), F32),
            pltpu.VMEM((RING, stat_rows, head), BF16),
            pltpu.VMEM((2, stat_rows // 2, head), BF16),
            pltpu.VMEM((2, stat_rows, head), BF16),
            dma((10,)), dma((7,)), dma((5, 3)), dma((5, 3)), dma((3,)), dma((3,)), dma((4,)), dma((4,)),
            dma((13,)), dma((13,)), dma((8,)), dma((8,)), dma((3,)), dma((3,)), dma((3,)), dma((3,)),
            dma((3,)), dma((3,)), dma((6,)), dma((6,)),
        ],
        compiler_params=pltpu.CompilerParams(
            collective_id=0, has_side_effects=True, vmem_limit_bytes=VMEM_LIMIT
        ),
    )(
        lengths.reshape(batches),
        upstream.reshape(rows, width),
        inputs.reshape(rows, head),
        in_proj[0],
        out_proj[0],
        in_inverse[0],
        out_inverse[0],
    )
    passed, precond, in_factor, out_factor = pl.pallas_call(
        store,
        out_shape=shapes,
        in_specs=[hbm] * 4,
        out_specs=(hbm,) * 4,
        scratch_shapes=[pltpu.VMEM(shape.shape, shape.dtype) for shape in shapes] + [dma((7,)), dma((7,))],
        compiler_params=pltpu.CompilerParams(vmem_limit_bytes=VMEM_LIMIT),
    )(*outs)
    return (passed.reshape(upstream.shape), precond[None], in_factor[None], out_factor[None])


def solution(mesh):
    in_specs = (
        P("section", None, "dp", None),
        P("section", None, "dp", None),
        P("section", "dp", None),
        P("section", "dp", None),
        P("section", None, None),
        P("section", "dp", None, None),
        P("section", "dp", None),
    )
    out_specs = (
        P("section", None, "dp", None),
        P("section", "dp", None),
        P("section", None, None),
        P("section", "dp", None, None),
    )
    return jax.shard_map(local, mesh=mesh, in_specs=in_specs, out_specs=out_specs, check_vma=False)
```

```python
import jax
import jax.numpy as jnp
from jax import lax
from jax.experimental import pallas as pl
from jax.experimental.pallas import tpu as pltpu
from jax.sharding import PartitionSpec as P

RING = 4
BF16 = jnp.bfloat16
F32 = jnp.float32
MESH = pl.DeviceIdType.MESH
VMEM_LIMIT = 56 * 1024 * 1024


def nt_dot(a, b):
    return lax.dot_general(a, b, (((1,), (1,)), ((), ())), preferred_element_type=F32)


def tn_dot(a, b):
    return lax.dot_general(a, b, (((0,), (0,)), ((), ())), preferred_element_type=F32)


def grid_of(shape):
    return lax.broadcasted_iota(jnp.int32, shape, 0), lax.broadcasted_iota(jnp.int32, shape, 1)


def pack_pair(first, second):
    row, column = grid_of(first.shape)
    return jnp.where(column > row, first, second)


def diagonal(matrix):
    row, column = grid_of(matrix.shape)
    return jnp.sum(jnp.where(column == row, matrix, 0.0), axis=0, keepdims=True)


def unpack_pair(packed, diagonal_row):
    row, column = grid_of(packed.shape)
    flipped = packed.T
    first = jnp.where(column > row, packed, jnp.where(column < row, flipped, diagonal_row))
    second = jnp.where(column > row, flipped, packed)
    return first, second


def kernel(
    lengths_hbm, upstream, inputs, in_proj, out_proj, in_inverse_hbm, out_inverse_hbm,
    passed_hbm, precond_hbm, in_factor_hbm, out_factor_hbm,
    passed, precond, in_factor, out_factor, lengths, raw, raw_values, raw_proj, in_inverse, out_inverse,
    sent, split, split_t, relayed, values, out_rows, in_rows, partial, partial_in, branch, branch_in,
    own_gram, gram_in, quarter, quarter_in, stats, half_in, stats_in,
    load, drain, split_send, split_recv, value_send, value_recv, out_send, out_recv,
    relay_send, relay_recv, in_send, in_recv, partial_send, partial_recv, gram_send, gram_recv,
    quarter_send, quarter_recv, stats_send, stats_recv,
):
    rows, width = upstream.shape
    slots = rows // lengths.shape[0]
    shard, head = in_proj.shape
    blocks, size, _ = out_inverse.shape
    span = RING * shard
    edge = size - head
    sections = lax.axis_size("section")
    dp = lax.axis_index("dp")
    section = lax.axis_index("section")
    x = lax.div(dp, RING)
    z = lax.rem(dp, RING)
    before = {"section": lax.rem(section + sections - 1, sections)}
    after = {"section": lax.rem(section + 1, sections)}

    def along_x(r):
        return {"dp": lax.rem(x + r, RING) * RING + z}

    def along_z(r):
        return {"dp": x * RING + lax.rem(z + r, RING)}

    started = []

    def send(src, dst, send_sem, recv_sem, device):
        copy = pltpu.make_async_remote_copy(
            src_ref=src, dst_ref=dst, send_sem=send_sem, recv_sem=recv_sem, device_id=device, device_id_type=MESH
        )
        copy.start()
        started.append(copy)
        return copy

    def fetch(src, dst, sem):
        copy = pltpu.make_async_copy(src, dst, sem)
        copy.start()
        return copy

    def span_at(r):
        return pl.ds(pl.multiple_of(lax.rem(x + r, RING) * span, head), span)

    def shard_at(device_x, device_z):
        return pl.ds(pl.multiple_of((device_x * RING + device_z) * shard, 16), shard)

    def half_shard(device_x, device_z, which):
        return pl.ds(pl.multiple_of((device_x * RING + device_z) * shard + which * (shard // 2), 16), shard // 2)

    barrier = pltpu.get_barrier_semaphore()
    for device in [along_x(r) for r in (1, 2, 3)] + [along_z(r) for r in (1, 2, 3)] + [before, after]:
        pl.semaphore_signal(barrier, inc=1, device_id=device, device_id_type=MESH)

    own_out = pl.ds(pl.multiple_of(z * shard, 16), shard)
    own_rows = fetch(out_proj, out_rows.at[own_out], load.at[6])
    own_proj = fetch(in_proj, raw_proj, load.at[9])
    loads = [fetch(lengths_hbm, lengths, load.at[0]), fetch(inputs, raw_values, load.at[1])]
    spans = {r: fetch(upstream.at[:, span_at(r)], raw.at[r], load.at[2 + r]) for r in (2, 1, 3, 0)}
    inverses = [fetch(in_inverse_hbm, in_inverse, load.at[7]), fetch(out_inverse_hbm, out_inverse, load.at[8])]

    for copy in loads:
        copy.wait()
    position = lax.broadcasted_iota(jnp.int32, (rows, 1), 0)
    batch = lax.div(position, slots)
    limit = jnp.where(batch == 0, lengths[0], jnp.where(batch == 1, lengths[1], lengths[2]))
    keep = (lax.rem(position, slots) < limit).astype(F32)
    keep = jnp.broadcast_to(keep, (rows, head)).astype(BF16)
    counted = (lengths[0] + lengths[1] + lengths[2]).astype(F32)
    values[0, 0:rows, :] = raw_values[...] * keep
    values[0, rows:, :] = jnp.full((16, head), counted, F32).astype(BF16)
    shared = (RING + 1) * head
    pair = 2 * head
    tile_at = [3 * p for p in range(RING + 1)] + [3 * k + 1 + j for k in range(RING) for j in range(2)]

    def mask(r):
        spans[r].wait()
        for p, tile in enumerate(tile_at):
            masked = raw[r, :, tile * head:(tile + 1) * head] * keep
            sent[r, :, p * head:(p + 1) * head] = masked
            if r == 0:
                split[0:rows, p * head:(p + 1) * head] = masked

    mask(2)

    pl.semaphore_wait(barrier, 8)

    own_rows.wait()
    own_proj.wait()
    out_a = send(out_rows.at[own_out], out_rows.at[own_out], out_send.at[0], out_recv.at[0], along_z(1))
    out_b = send(out_rows.at[own_out], out_rows.at[own_out], out_send.at[1], out_recv.at[1], along_z(3))
    own_in = shard_at(x, z)
    in_first = send(raw_proj, in_rows.at[own_in], in_send.at[0], in_recv.at[0], before)

    vals = [send(values.at[0], values.at[r], value_send.at[r - 1], value_recv.at[r - 1], along_x(r)) for r in (1, 2, 3)]

    def pair_at(step):
        return pl.ds(pl.multiple_of(shared + lax.rem(z + step, RING) * pair, head), pair)

    def scatter(step, r):
        where = pl.ds(0, shared) if step is None else pair_at(step)
        at = 0 if step is None else step + 1
        return send(
            sent.at[r, :, where], split.at[pl.ds(r * rows, rows), where],
            split_send.at[at, r - 1], split_recv.at[at, r - 1], along_x(r),
        )

    splits = {}
    for r in (2, 1, 3):
        if r != 2:
            mask(r)
        splits[None, r] = scatter(None, r)
    for r in (2, 1, 3):
        splits[2, r] = scatter(2, r)
    mask(0)
    for step in (1, 3, 0):
        for r in (2, 1, 3):
            splits[step, r] = scatter(step, r)

    def arrived(step):
        for r in (1, 3, 2):
            splits[step, r].wait_recv()

    cuts = ((0, shared), (shared, 2 * pair), (shared + 2 * pair, 2 * pair))
    relays = {}

    for piece in range(12):
        r, cut = (0, 3, 1, 2)[piece // 3], piece % 3
        where = pl.ds(*cuts[cut])
        relays[r, cut] = pltpu.make_async_remote_copy(
            src_ref=sent.at[r, :, where], dst_ref=relayed.at[r, :, where], send_sem=relay_send.at[piece],
            recv_sem=relay_recv.at[piece], device_id=before, device_id_type=MESH,
        )
    started += relays.values()
    same_chip = lax.rem(section, 2)

    def relay(parity):
        @pl.when(same_chip == parity)
        def _():
            for copy in relays.values():
                copy.start()

    in_first.wait_recv()
    in_a = send(in_rows.at[own_in], in_rows.at[own_in], in_send.at[1], in_recv.at[1], along_z(1))
    in_b = send(in_rows.at[own_in], in_rows.at[own_in], in_send.at[2], in_recv.at[2], along_z(3))
    left, right = lax.rem(z + 3, RING), lax.rem(z + 1, RING)
    half = shard // 2
    low = pl.ds(pl.multiple_of(left * shard, 16), half)
    high = pl.ds(pl.multiple_of(right * shard + half, 16), half)
    out_a.wait_recv()
    out_c = send(out_rows.at[low], out_rows.at[low], out_send.at[2], out_recv.at[2], along_z(1))
    out_b.wait_recv()
    out_d = send(out_rows.at[high], out_rows.at[high], out_send.at[3], out_recv.at[3], along_z(3))

    for copy in vals:
        copy.wait_recv()
    stacked = jnp.concatenate([values[r, 0:rows, :] for r in range(RING)], axis=0)
    quart = head // RING
    own_gram[...] = tn_dot(stacked, stacked).astype(BF16)
    gram_in[0, 0:quart, :] = own_gram[pl.ds(pl.multiple_of(x * quart, 16), quart), :]
    count_row = lax.broadcasted_iota(jnp.int32, (16, head), 0)
    counts = jnp.zeros((16, head), F32)
    for r in range(RING):
        counts = jnp.where(count_row == r, values[r, rows:, :].astype(F32), counts)
    gram_in[0, quart:, :] = counts.astype(BF16)
    grams = [send(gram_in.at[0], gram_in.at[r], gram_send.at[r - 1], gram_recv.at[r - 1], along_z(r)) for r in (1, 2, 3)]

    in_a.wait_recv()
    low_in = half_shard(x, left, 0)
    in_c = send(in_rows.at[low_in], in_rows.at[low_in], in_send.at[3], in_recv.at[3], along_z(1))
    in_b.wait_recv()
    high_in = half_shard(x, right, 1)
    in_d = send(in_rows.at[high_in], in_rows.at[high_in], in_send.at[4], in_recv.at[4], along_z(3))

    arrived(None)
    for p in range(RING + 1):
        split_t[3 * p * head:(3 * p + 1) * head, :] = split[:, p * head:(p + 1) * head].T

    def turn(step):
        first = (3 * lax.rem(z + step, RING) + 1) * head
        split_t[pl.ds(pl.multiple_of(first, head), pair), :] = split[:, pair_at(step)].T

    at_edge = head
    at_corner = at_edge + blocks * edge
    at_diagonal = at_corner + edge
    at_weight = at_diagonal + 16
    diagonal_row = lax.broadcasted_iota(jnp.int32, (16, head), 0)

    def statistics(r):
        owner = lax.rem(z + r, RING) * shard
        grams = []
        for b in range(blocks):
            g = split_t[pl.ds(pl.multiple_of(owner + b * size, 16), size), :]
            grams.append(nt_dot(g, g))
            stats[r, at_edge + b * edge:at_edge + (b + 1) * edge, :] = grams[b][head:, 0:head].astype(BF16)
        stats[r, 0:head, :] = pack_pair(grams[0][0:head, 0:head], grams[1][0:head, 0:head]).astype(BF16)
        corner = pack_pair(grams[0][head:, head:], grams[1][head:, head:])
        stats[r, at_corner:at_diagonal, 0:edge] = corner.astype(BF16)
        first = diagonal(grams[0][0:head, 0:head])
        stats[r, at_diagonal:at_weight, :] = jnp.where(diagonal_row == 0, first, 0.0).astype(BF16)
        second = diagonal(grams[0][head:, head:])
        stats[r, at_diagonal:at_weight, 0:edge] = jnp.where(
            diagonal_row[:, 0:edge] == 0, first[:, 0:edge], jnp.where(diagonal_row[:, 0:edge] == 1, second, 0.0)
        ).astype(BF16)
        weight = jnp.dot(
            split_t[pl.ds(pl.multiple_of(owner, 16), shard), :], stacked, preferred_element_type=F32
        )
        stats[r, at_weight:, :] = weight.astype(BF16)

    stat_rows = stats.shape[1]
    cut = stat_rows // 2
    top, bottom = pl.ds(0, cut), pl.ds(cut, cut)
    arrived(2)
    turn(2)
    statistics(2)
    half_a = send(stats.at[2, top], half_in.at[0], stats_send.at[0], stats_recv.at[0], along_z(1))
    half_b = send(stats.at[2, bottom], half_in.at[1], stats_send.at[1], stats_recv.at[1], along_z(3))
    for copy in grams:
        copy.wait_recv()
    total = gram_in[0].astype(F32)
    for r in (1, 2, 3):
        total = total + gram_in[r].astype(F32)
    count = jnp.sum(total[quart:, :], axis=0, keepdims=True)
    quarter[...] = total[0:quart, :] / count
    count = count[:, 0:1]
    quarters = [
        send(quarter, quarter_in.at[r - 1], quarter_send.at[r - 1], quarter_recv.at[r - 1], along_x(r)) for r in (1, 2, 3)
    ]

    arrived(1)
    turn(1)
    statistics(1)
    near_b = send(stats.at[1, bottom], stats_in.at[0, bottom], stats_send.at[2], stats_recv.at[2], along_z(1))
    arrived(3)
    turn(3)
    statistics(3)
    near_a = send(stats.at[3, top], stats_in.at[1, top], stats_send.at[3], stats_recv.at[3], along_z(3))
    arrived(0)
    out_c.wait_recv()
    out_d.wait_recv()
    ordered = [out_rows[3 * p * head:(3 * p + 1) * head, :] for p in range(RING + 1)]
    ordered += [out_rows[(3 * k + 1) * head:(3 * k + 3) * head, :] for k in range(RING)]
    part = jnp.dot(split[...], jnp.concatenate(ordered, axis=0), preferred_element_type=F32)
    partial[...] = part
    partials = [
        send(
            partial.at[pl.ds(r * rows, rows)], partial_in.at[r - 1],
            partial_send.at[r - 1], partial_recv.at[r - 1], along_x(RING - r),
        )
        for r in (1, 2, 3)
    ]

    in_c.wait_recv()
    in_d.wait_recv()
    own_span = pl.ds(pl.multiple_of(x * span, 16), span)
    in_x = [
        send(in_rows.at[own_span], in_rows.at[own_span], in_send.at[4 + r], in_recv.at[4 + r], along_x(r))
        for r in (1, 3, 2)
    ]

    half_a.wait_recv()
    stats[1, top, :] = (stats[1, top, :].astype(F32) + half_in[0].astype(F32)).astype(BF16)
    far_a = send(stats.at[1, top], stats_in.at[0, top], stats_send.at[4], stats_recv.at[4], along_z(1))
    half_b.wait_recv()
    stats[3, bottom, :] = (stats[3, bottom, :].astype(F32) + half_in[1].astype(F32)).astype(BF16)
    far_b = send(stats.at[3, bottom], stats_in.at[1, bottom], stats_send.at[5], stats_recv.at[5], along_z(3))

    turn(0)
    statistics(0)
    total = part[0:rows, :]
    for r in (1, 2, 3):
        partials[r - 1].wait_recv()
        total = total + partial_in[r - 1]
    branch[...] = total.astype(BF16)
    branches = send(branch, branch_in, relay_send.at[12], relay_recv.at[12], before)
    near_a.wait_recv()
    near_b.wait_recv()
    relay(0)

    in_factor[pl.ds(pl.multiple_of(x * quart, 16), quart), :] = quarter[...]
    for r in (1, 2, 3):
        quarters[r - 1].wait_recv()
        source = lax.rem(x + RING - r, RING)
        in_factor[pl.ds(pl.multiple_of(source * quart, 16), quart), :] = quarter_in[r - 1]
    drained = [fetch(in_factor, in_factor_hbm, drain.at[0])]

    for copy in (far_a, far_b):
        copy.wait_recv()
    relay(1)
    for copy in inverses:
        copy.wait()
    total = stats[0].astype(F32) + stats_in[0].astype(F32) + stats_in[1].astype(F32)
    heads = unpack_pair(total[0:head, :], total[at_diagonal:at_diagonal + 1, :])
    corners = unpack_pair(total[at_corner:at_diagonal, 0:edge], total[at_diagonal + 1:at_diagonal + 2, 0:edge])
    for b in range(blocks):
        side = total[at_edge + b * edge:at_edge + (b + 1) * edge, :] / count
        out_factor[b, 0:head, 0:head] = heads[b] / count
        out_factor[b, head:, 0:head] = side
        out_factor[b, 0:head, head:] = side.T
        out_factor[b, head:, head:] = corners[b] / count
        weight = total[at_weight + b * size:at_weight + (b + 1) * size, :] / jnp.sqrt(count)
        left_product = jnp.dot(out_inverse[b], weight, precision=lax.Precision.HIGHEST, preferred_element_type=F32)
        precond[b * size:(b + 1) * size, :] = jnp.dot(
            left_product, in_inverse[...], precision=lax.Precision.HIGHEST, preferred_element_type=F32
        )

    drained += [fetch(precond, precond_hbm, drain.at[1]), fetch(out_factor, out_factor_hbm, drain.at[2])]

    branches.wait_recv()
    scale = jnp.where(section == sections - 1, 0.0, 1.0).astype(F32)
    for copy, r in zip([None] + in_x, (0, 3, 1, 2)):
        if copy is not None:
            copy.wait_recv()
        first = lax.rem(x + r, RING) * span
        for cut, (start, extent) in enumerate(cuts):
            relays[r, cut].wait_recv()
            step = head if cut == 0 else pair
            for at in range(start, start + extent, step):
                columns = pl.ds(pl.multiple_of(first + tile_at[at // head] * head, head), step)
                sums = relayed[r, :, at:at + step].astype(F32) + nt_dot(branch_in[...], in_rows[columns, :])
                passed[:, columns] = (sums * scale).astype(BF16)
        drained.append(fetch(passed.at[:, span_at(r)], passed_hbm.at[:, span_at(r)], drain.at[3 + r]))

    for copy in started:
        copy.wait_send()
    for copy in drained:
        copy.wait()


def store(*refs):
    sources, targets, held, arrive, leave = refs[:4], refs[4:8], refs[8:12], refs[12], refs[13]
    width = sources[0].shape[1]
    piece = width // 4
    views = [lambda ref, i=i: ref.at[:, pl.ds(i * piece, piece)] for i in range(4)]
    parts = [(view(sources[0]), view(held[0]), view(targets[0])) for view in views]
    parts += list(zip(sources[1:], held[1:], targets[1:]))
    loads = [pltpu.make_async_copy(part[0], part[1], arrive.at[i]) for i, part in enumerate(parts)]
    stores = [pltpu.make_async_copy(part[1], part[2], leave.at[i]) for i, part in enumerate(parts)]
    for copy in loads:
        copy.start()
    for load, copy in zip(loads, stores):
        load.wait()
        copy.start()
    for copy in stores:
        copy.wait()


def local(upstream, inputs, in_proj, out_proj, in_inverse, out_inverse, lengths):
    _, batches, slots, width = upstream.shape
    rows = batches * slots
    head = inputs.shape[3]
    shard = in_proj.shape[1]
    blocks, size = out_inverse.shape[1:3]
    span = RING * shard
    edge = size - head
    stat_rows = head + blocks * edge + edge + 16 + shard
    hbm = pl.BlockSpec(memory_space=pltpu.HBM)
    dma = pltpu.SemaphoreType.DMA
    shapes = (
        jax.ShapeDtypeStruct((rows, width), BF16),
        jax.ShapeDtypeStruct((shard, head), F32),
        jax.ShapeDtypeStruct((head, head), F32),
        jax.ShapeDtypeStruct((blocks, size, size), F32),
    )
    outs = pl.pallas_call(
        kernel,
        out_shape=shapes,
        in_specs=[hbm] * 7,
        out_specs=(hbm,) * 4,
        scratch_shapes=[
            pltpu.VMEM((rows, width), BF16),
            pltpu.VMEM((shard, head), F32),
            pltpu.VMEM((head, head), F32),
            pltpu.VMEM((blocks, size, size), F32),
            pltpu.SMEM((batches,), jnp.int32),
            pltpu.VMEM((RING, rows, span), BF16),
            pltpu.VMEM((rows, head), BF16),
            pltpu.VMEM((shard, head), BF16),
            pltpu.VMEM((head, head), F32),
            pltpu.VMEM((blocks, size, size), F32),
            pltpu.VMEM((RING, rows, span), BF16),
            pltpu.VMEM((RING * rows, span), BF16),
            pltpu.VMEM((span, RING * rows), BF16),
            pltpu.VMEM((RING, rows, span), BF16),
            pltpu.VMEM((RING, rows + 16, head), BF16),
            pltpu.VMEM((span, head), BF16),
            pltpu.VMEM((width, head), BF16),
            pltpu.VMEM((RING * rows, head), F32),
            pltpu.VMEM((RING - 1, rows, head), F32),
            pltpu.VMEM((rows, head), BF16),
            pltpu.VMEM((rows, head), BF16),
            pltpu.VMEM((head, head), BF16),
            pltpu.VMEM((RING, head // RING + 16, head), BF16),
            pltpu.VMEM((head // RING, head), F32),
            pltpu.VMEM((RING - 1, head // RING, head), F32),
            pltpu.VMEM((RING, stat_rows, head), BF16),
            pltpu.VMEM((2, stat_rows // 2, head), BF16),
            pltpu.VMEM((2, stat_rows, head), BF16),
            dma((10,)), dma((7,)), dma((5, 3)), dma((5, 3)), dma((3,)), dma((3,)), dma((4,)), dma((4,)),
            dma((13,)), dma((13,)), dma((8,)), dma((8,)), dma((3,)), dma((3,)), dma((3,)), dma((3,)),
            dma((3,)), dma((3,)), dma((6,)), dma((6,)),
        ],
        compiler_params=pltpu.CompilerParams(
            collective_id=0, has_side_effects=True, vmem_limit_bytes=VMEM_LIMIT
        ),
    )(
        lengths.reshape(batches),
        upstream.reshape(rows, width),
        inputs.reshape(rows, head),
        in_proj[0],
        out_proj[0],
        in_inverse[0],
        out_inverse[0],
    )
    passed, precond, in_factor, out_factor = pl.pallas_call(
        store,
        out_shape=shapes,
        in_specs=[hbm] * 4,
        out_specs=(hbm,) * 4,
        scratch_shapes=[pltpu.VMEM(shape.shape, shape.dtype) for shape in shapes] + [dma((7,)), dma((7,))],
        compiler_params=pltpu.CompilerParams(vmem_limit_bytes=VMEM_LIMIT),
    )(*outs)
    return (passed.reshape(upstream.shape), precond[None], in_factor[None], out_factor[None])


def solution(mesh):
    in_specs = (
        P("section", None, "dp", None),
        P("section", None, "dp", None),
        P("section", "dp", None),
        P("section", "dp", None),
        P("section", None, None),
        P("section", "dp", None, None),
        P("section", "dp", None),
    )
    out_specs = (
        P("section", None, "dp", None),
        P("section", "dp", None),
        P("section", None, None),
        P("section", "dp", None, None),
    )
    return jax.shard_map(local, mesh=mesh, in_specs=in_specs, out_specs=out_specs, check_vma=False)
```
